32 devices in a mesh: seq: 16 (over z, y, x), tp: 2 (over core).
Axes of the slice: x: 2, y: 2, z: 4, core: 2. Of those that a mesh axis runs over, the one named last changes fastest.
Arguments:
- features: float32 [3, 4096, 4096], P(None, 'tp', 'seq'), may hold values from -6 to 6
- short_filter: float32 [3, 256, 7], P(None, 'tp'), may hold values from -2 to 2
- medium_filter: float32 [3, 256, 128], P(None, 'tp'), may hold values from -0.5 to 0.5
- rates: float32 [256, 16], P('tp'), as said below
- residues: float32 [256, 16], P('tp'), may hold values from -1.5 to 1.5
- skip_gain: float32 [4096], P('tp'), may hold values from -4 to 4
- out_weight: bfloat16 [2048, 4096], P(None, 'tp'), may hold values from -0.125 to 0.125
Outputs:
- mixed: float32 [2048, 4096], P('tp', 'seq')
The draws below stay inside these ranges and needn't reach their ends.
Inputs may be any that keep to these rules, and one draw needn't show every extreme that they name: `rates`: every rate lies between 1 / 40960 and 1 / 20.
All inputs are finite; a program needn't handle non-finite values.
Results may differ from the reference program's by a relative error of at most 0.0029.
Values sent between devices are 32-bit elements; how exact they have to be, the bound alone decides.
No kernel may reach another device: no remote copies, remote signals or barrier semaphores. Data moves between devices by JAX's collectives and lax.ppermute only.
A program may use at most 128 MiB of HBM per device.

```python
import math
import jax
import jax.numpy as jnp
from jax import lax

D = 4096
D_OUT = 2048
GROUP = 16
SHORT = 7
MEDIUM = 128
ORDER = 16
T_DEV = 256
TOKENS = 4096


def draw_rates(key, part):
    key_class, key_level = jax.random.split(jax.random.fold_in(key, 17), 2)
    shape = (D // GROUP, ORDER)
    picker = jax.random.uniform(key_class, shape, jnp.float32)
    level = jax.random.uniform(key_level, shape, jnp.float32)
    slow_rate = jnp.exp(math.log(0.1 / TOKENS) + level * math.log(20.0))
    fast_rate = jnp.exp(math.log(0.02) + level * math.log(2.5))
    middle_rate = jnp.exp(math.log(0.25 / T_DEV) + level * math.log(16.0))
    chosen = jnp.where(picker < 0.3, fast_rate, jnp.where(picker < 0.5, middle_rate, slow_rate))
    return chosen.astype(jnp.float32)


def spiked(values, stream_key, source, target, parts, factor):
    owner, partner = [(jnp.arange(values.shape[axis_at]) // (values.shape[axis_at] // parts)).reshape([-1 if axis == axis_at else 1 for axis in range(values.ndim)]) for axis_at in (source, target)]
    chosen = jax.random.permutation(stream_key, parts)[partner]
    strong = (owner == chosen) | (owner == (partner + parts // 2) % parts)
    return jnp.where(strong, factor * values, values)


def block_levels(rng, dims, cuts, low, top_value):
    def one(dim, parts):
        steps = jax.random.uniform(jax.random.fold_in(jax.random.fold_in(rng, 6), dim), (parts,), jnp.float32, low / len(cuts), top_value / len(cuts))
        return jnp.repeat(jnp.exp(steps), dims[dim] // parts).reshape((-1,) + (1,) * (len(dims) - dim - 1))

    loudness = one(*cuts[0])
    for cut in cuts[1:]:
        loudness = loudness * one(*cut)
    return loudness


def bell_draw(stream_key, extent, scale, reach, pieces=(), kind=jnp.bfloat16):
    values = jax.random.normal(stream_key, extent, jnp.float32) * scale
    if len(pieces) > 0:
        values = block_levels(stream_key, extent, pieces, -0.22, 0.18) * values
    return jnp.clip(values, min=-reach, max=reach).astype(kind)


def noise_with(stream_key, extent, spread, bound, shards, heavy, kind=jnp.bfloat16):
    array = spread * jax.random.normal(stream_key, extent, jnp.float32)
    if shards:
        array = array * block_levels(stream_key, extent, shards, -0.22, 0.18)
    return jnp.clip(spiked(array, jax.random.fold_in(stream_key, 3), *heavy), -bound, bound).astype(kind)


def setup_inputs(seed: int = 0) -> dict:
    streams_of = jax.random.split(jax.random.key(seed), 8)
    return {
        "features": bell_draw(streams_of[0], (3, D, TOKENS), 1.0, 6.0, ((1, 2), (2, 16)), jnp.float32),
        "short_filter": bell_draw(streams_of[1], (3, D // GROUP, SHORT), SHORT ** -0.5, 2.0, ((1, 2),), jnp.float32),
        "medium_filter": bell_draw(streams_of[2], (3, D // GROUP, MEDIUM), MEDIUM ** -0.5, 0.5, ((1, 2),), jnp.float32),
        "rates": draw_rates(jax.random.fold_in(streams_of[7], 71), 0),
        "residues": bell_draw(streams_of[4], (D // GROUP, ORDER), 0.25, 1.5, ((0, 2),), jnp.float32),
        "skip_gain": bell_draw(streams_of[5], (D,), 1.0, 4.0, ((0, 2),), jnp.float32),
        "out_weight": noise_with(streams_of[6], (D_OUT, D), D ** -0.5, 0.125, ((1, 2),), (1, 0, 2, 2.0)),
    }


def short_conv(extended, filters, length):
    coeffs = jnp.repeat(filters, GROUP, axis=1)
    summed = jnp.zeros(extended.shape[:-1] + (length,), extended.dtype)
    for offset in range(SHORT):
        first = SHORT - 1 - offset
        summed = summed + coeffs[:, :, offset:offset + 1] * extended[:, :, first:first + length]
    return summed

def medium_matrix(coeffs):
    block_len = coeffs.shape[0]
    pattern = jnp.concatenate([coeffs[::-1], jnp.zeros((block_len,), coeffs.dtype)])
    return jnp.tile(pattern, block_len)[:block_len * (2 * block_len - 1)].reshape(block_len, 2 * block_len - 1)

def medium_branch(operands):
    extended, coeffs = operands
    block_len = coeffs.shape[1]
    channels = extended.shape[0]
    groups = coeffs.shape[0]
    length = extended.shape[1] - (block_len - 1)
    block_count = length // block_len
    padded = jnp.concatenate([jnp.zeros((channels, 1), extended.dtype), extended], axis=1)
    blocks = padded.reshape(channels, block_count + 1, block_len)
    windows = jnp.concatenate([blocks[:, :-1], blocks[:, 1:]], axis=2)[:, :, 1:]
    windows = windows.reshape(groups, channels // groups, block_count, 2 * block_len - 1)
    matrices = jax.vmap(medium_matrix)(coeffs)
    result = jnp.einsum('gcbs,gts->gcbt', windows, matrices, precision=lax.Precision.HIGHEST)
    return result.reshape(channels, length)

def long_matrix(kernel):
    block_len = kernel.shape[0]
    pattern = jnp.concatenate([kernel[0:1], jnp.zeros((block_len,), kernel.dtype), kernel[1:][::-1]])
    full = jnp.tile(pattern, block_len)[:block_len * (2 * block_len - 1)].reshape(block_len, 2 * block_len - 1)
    return full[:, :block_len]

def modal_tables(rates, residues, block_len):
    steps_axis = jnp.arange(block_len).astype(rates.dtype)
    weight = residues * jnp.sqrt(-jnp.expm1(-2.0 * rates))
    decays = jnp.exp(-rates[:, :, None] * steps_axis)
    kernel = jnp.einsum('gn,gnt->gt', weight, decays, precision=lax.Precision.HIGHEST)
    readout = weight[:, :, None] * jnp.exp(-rates[:, :, None] * (steps_axis + 1.0))
    ending = decays[:, :, ::-1]
    return (kernel, readout, ending)

def long_conv(product, rates, residues):
    block_len = MEDIUM
    groups = rates.shape[0]
    kernel, readout, ending = modal_tables(rates, residues, block_len)
    matrices = jax.vmap(long_matrix)(kernel)
    block_count = TOKENS // block_len
    blocks = product.reshape(groups, GROUP, block_count, block_len).transpose(2, 0, 1, 3)
    step_decay = jnp.exp(-rates * block_len)

    def advance(states, block):
        inside = jnp.einsum('gcs,gts->gct', block, matrices, precision=lax.Precision.HIGHEST)
        carried = jnp.einsum('gcn,gnt->gct', states, readout, precision=lax.Precision.HIGHEST)
        finals = jnp.einsum('gcs,gns->gcn', block, ending, precision=lax.Precision.HIGHEST)
        return (step_decay[:, None, :] * states + finals, inside + carried)
    start_states = jnp.zeros((groups, GROUP, ORDER), product.dtype)
    unused, outputs = lax.scan(advance, start_states, blocks)
    return outputs.transpose(1, 2, 0, 3).reshape(groups * GROUP, TOKENS)

def reference(features, short_filter, medium_filter, rates, residues, skip_gain, out_weight):
    padded = jnp.pad(features, ((0, 0), (0, 0), (SHORT - 1, 0)))
    shorted = short_conv(padded, short_filter, TOKENS)
    extended = jnp.pad(shorted, ((0, 0), (0, 0), (MEDIUM - 1, 0)))
    mediated = lax.map(medium_branch, (extended, medium_filter))
    product = mediated[1] * mediated[2]
    longed = long_conv(product, rates, residues) + skip_gain[:, None] * product
    gated = (mediated[0] * longed).astype(jnp.bfloat16)
    gated = lax.optimization_barrier(gated)
    return jnp.dot(out_weight.astype(jnp.float32), gated.astype(jnp.float32), precision=lax.Precision.HIGHEST)
```

```python
import functools

import jax
import jax.numpy as jnp
import numpy as np
from jax import lax
from jax.experimental import pallas as pl
from jax.experimental.pallas import tpu as pltpu
from jax.sharding import PartitionSpec as P

GROUP = 16
SHORT = 7
MEDIUM = 128
ORDER = 16
LANES = 128
BLOCK = 256
GROUPS = BLOCK // GROUP
BORDER = 16
ROWS = BLOCK + BORDER
VMEM_LIMIT = 40 * 1024 * 1024
BF16 = jnp.bfloat16
F32 = jnp.float32


def split_np(x):
    import_type = jnp.bfloat16
    hi = x.astype(np.float32).astype(import_type)
    lo = (x - hi.astype(np.float64)).astype(np.float32).astype(import_type)
    return hi, lo


def transforms():
    n = 2 * MEDIUM
    s = np.arange(n)[:, None]
    k = np.arange(MEDIUM)[None, :]
    angle = np.pi * (((2 * k + 1) * s) % (2 * n)) / n
    fwd = np.concatenate([np.cos(angle), -np.sin(angle)], axis=1)
    inv = (2.0 / n) * np.concatenate([np.cos(angle), -np.sin(angle)], axis=1).T[:, MEDIUM:]
    return fwd, inv


def stacked(x):
    hi, lo = split_np(x)
    return np.concatenate([hi, hi, lo], axis=0)


def split(x):
    hi = x.astype(BF16)
    lo = (x - hi.astype(F32)).astype(BF16)
    return hi, lo


def split_3(x):
    hi = x.astype(BF16)
    rest = x - hi.astype(F32)
    mid = rest.astype(BF16)
    low = (rest - mid.astype(F32)).astype(BF16)
    return hi, mid, low


def dot(a, b):
    return jnp.dot(a, b, preferred_element_type=F32)


def dot_3(x, stack):
    hi, lo = split(x)
    return dot(jnp.concatenate([hi, lo, hi], axis=1), stack)


def taps(before, now, coeff, count):
    lane = lax.broadcasted_iota(jnp.int32, now.shape, 1)
    total = coeff(0) * now
    for j in range(1, count):
        total = total + coeff(j) * pltpu.roll(jnp.where(lane >= LANES - j, before, now), j, 1)
    return total


def send_kernel(first_group, taps_ref, x_ref, out_ref):
    step = pl.program_id(0)
    for g in range(GROUPS):
        rows = slice(g * GROUP, (g + 1) * GROUP)
        base = first_group(step) + g
        out_ref[rows, :] = taps(
            x_ref[0, rows, :LANES],
            x_ref[0, rows, LANES:],
            lambda j: taps_ref[base * SHORT + j],
            SHORT,
        )
    for b in range(BLOCK // LANES):
        tile = x_ref[0, b * LANES : (b + 1) * LANES, LANES:]
        out_ref[BLOCK + 8 * b : BLOCK + 8 * (b + 1), :] = tile.T[LANES - 8 :]


def send_call(features, taps_flat, branches, first, width):
    per = width // BLOCK
    groups_all = features.shape[1] // GROUP

    def branch(step):
        return branches[0] + step // per

    def first_group(step):
        return branch(step) * groups_all + (first // BLOCK + step % per) * GROUPS

    steps = per * len(branches)
    return pl.pallas_call(
        functools.partial(send_kernel, first_group),
        grid=(steps,),
        in_specs=[
            pl.BlockSpec(memory_space=pltpu.SMEM),
            pl.BlockSpec(
                (1, BLOCK, 2 * LANES), lambda i: (branch(i), first // BLOCK + i % per, 0)
            ),
        ],
        out_specs=pl.BlockSpec((ROWS, LANES), lambda i: (i, 0)),
        out_shape=jax.ShapeDtypeStruct((steps * ROWS, LANES), F32),
        compiler_params=pltpu.CompilerParams(vmem_limit_bytes=VMEM_LIMIT),
        cost_estimate=pl.CostEstimate(
            flops=steps * BLOCK * LANES * 14,
            bytes_accessed=steps * (BLOCK * 3 + BORDER) * LANES * 4,
            transcendentals=0,
        ),
        name="send",
    )(taps_flat, features)


def filtered(response, freq_ref, prod_ref, inv, repeats):
    for g in range(GROUPS):
        spectrum = response(g)
        hr, hi = spectrum[:, :LANES], spectrum[:, LANES:]
        for r in range(repeats):
            rows = slice(r * BLOCK + g * GROUP, r * BLOCK + (g + 1) * GROUP)
            xr, xi = freq_ref[rows, :LANES], freq_ref[rows, LANES:]
            yr = xr * hr - xi * hi
            yi = xr * hi + xi * hr
            yr_hi, yr_lo = split(yr)
            yi_hi, yi_lo = split(yi)
            prod_ref[rows, 0:128] = yr_hi
            prod_ref[rows, 128:256] = yi_hi
            prod_ref[rows, 256:384] = yr_lo
            prod_ref[rows, 384:512] = yi_lo
            prod_ref[rows, 512:640] = yr_hi
            prod_ref[rows, 640:768] = yi_hi
    return dot(prod_ref[...], inv)


def mediate(halo_ref, own_ref, x_ref, taps_ref, group, h_ref, place, fwd, inv, scratch):
    first_ref, freq_ref, prod_ref = scratch
    row = lax.broadcasted_iota(jnp.int32, (24, LANES), 0)
    lane = lax.broadcasted_iota(jnp.int32, (24, LANES), 1)
    select = (lane - (LANES - 8) == row % 8).astype(F32).astype(BF16)
    for b in range(BLOCK // LANES):
        border = halo_ref[BLOCK + 8 * b : BLOCK + 8 * (b + 1), :]
        pieces = jnp.concatenate([p.astype(F32) for p in split_3(border)], axis=0).astype(BF16)
        first_ref[b * LANES : (b + 1) * LANES, :] = lax.dot_general(
            pieces, select, (((0,), (0,)), ((), ())), preferred_element_type=F32
        )
    for g in range(GROUPS):
        rows = slice(g * GROUP, (g + 1) * GROUP)
        base = group + g
        first_ref[rows, :] = taps(
            first_ref[rows, :], x_ref[0, rows, :], lambda j: taps_ref[base * SHORT + j], SHORT
        )
    middle = first_ref[...]
    windows = jnp.concatenate(
        [
            jnp.concatenate([halo_ref[:BLOCK, :], middle], axis=1),
            jnp.concatenate([middle, own_ref[:BLOCK, :]], axis=1),
        ],
        axis=0,
    )
    freq_ref[...] = dot_3(windows, fwd)
    return filtered(lambda g: h_ref[place, g : g + 1, :], freq_ref, prod_ref, inv, 2)


def same_group():
    row = lax.broadcasted_iota(jnp.int32, (BLOCK, BLOCK), 0)
    lane = lax.broadcasted_iota(jnp.int32, (BLOCK, BLOCK), 1)
    return row // GROUP == lane // ORDER


def selector(rows):
    row = lax.broadcasted_iota(jnp.int32, (rows, BLOCK), 0)
    lane = lax.broadcasted_iota(jnp.int32, (rows, BLOCK), 1)
    return (lane % ORDER == row % ORDER).astype(F32).astype(BF16)


def pair_kernel(
    group_of, taps_ref, halo_k, halo_v, own_k, own_v, x_k, x_v, h_ref, hk_ref, fwd_ref, inv_ref,
    end_hi, end_lo, read_hi, read_lo, decay_ref, skip_ref, local_ref, state_ref,
    first_ref, freq_ref, prod_ref,
):
    step = pl.program_id(0)
    fwd, inv = fwd_ref[...], inv_ref[...]
    scratch = (first_ref, freq_ref, prod_ref)
    key = mediate(halo_k, own_k, x_k, taps_ref, group_of(1, step), h_ref, 0, fwd, inv, scratch)
    value = mediate(halo_v, own_v, x_v, taps_ref, group_of(2, step), h_ref, 1, fwd, inv, scratch)
    product = key * value
    hi, lo = split(product)
    terms = jnp.concatenate([hi, lo, hi], axis=1)
    half = MEDIUM
    late = jnp.concatenate(
        [fwd_ref[half : 2 * half], fwd_ref[half : 2 * half], fwd_ref[5 * half : 6 * half]], axis=0
    )
    freq_ref[...] = dot(terms, late)
    local = filtered(lambda g: hk_ref[g : g + 1, :], freq_ref, prod_ref, inv, 2)
    skip = jnp.concatenate([skip_ref[...], skip_ref[...]], axis=0)
    local = local + skip * product
    ends = dot(terms, jnp.concatenate([end_hi[...], end_hi[...], end_lo[...]], axis=0))
    mask = same_group()
    end_0 = jnp.where(mask, ends[:BLOCK], 0.0)
    end_1 = jnp.where(mask, ends[BLOCK:], 0.0)
    read = jnp.concatenate(
        [read_hi[:, :LANES], read_hi[:, :LANES], read_lo[:, :LANES]], axis=0
    )
    local_ref[:, :LANES] = local[:BLOCK]
    local_ref[:, LANES:] = local[BLOCK:] + dot_3(end_0, read)
    state = jnp.concatenate(split_3(end_0 * decay_ref[...] + end_1), axis=1)
    pick = selector(ORDER)
    state_ref[...] = lax.dot_general(
        jnp.concatenate([pick, pick, pick], axis=1),
        state,
        (((1,), (1,)), ((), ())),
        preferred_element_type=F32,
    )


def const_spec(shape):
    return pl.BlockSpec(shape, lambda i: (0,) * len(shape))


def pair_call(taps_flat, halo, own, features, spectra, long_spectra, fwd, inv, tables, first, width):
    per = width // BLOCK
    at = first // BLOCK
    groups_all = features.shape[1] // GROUP
    ends_hi, ends_lo, read_hi, read_lo, decay, skip = tables

    def group_of(branch, step):
        return branch * groups_all + (at + step) * GROUPS

    buffers = [
        pl.BlockSpec((ROWS, LANES), lambda i: (i, 0)),
        pl.BlockSpec((ROWS, LANES), lambda i: (per + i, 0)),
    ]
    return pl.pallas_call(
        functools.partial(pair_kernel, group_of),
        grid=(per,),
        in_specs=[
            pl.BlockSpec(memory_space=pltpu.SMEM),
            *buffers,
            *buffers,
            pl.BlockSpec((1, BLOCK, LANES), lambda i: (1, at + i, 0)),
            pl.BlockSpec((1, BLOCK, LANES), lambda i: (2, at + i, 0)),
            pl.BlockSpec((2, GROUPS, 2 * LANES), lambda i: (0, at + i, 0)),
            pl.BlockSpec((GROUPS, 2 * LANES), lambda i: (at + i, 0)),
            const_spec(fwd.shape),
            const_spec(inv.shape),
            pl.BlockSpec((MEDIUM, BLOCK), lambda i: (0, at + i)),
            pl.BlockSpec((MEDIUM, BLOCK), lambda i: (0, at + i)),
            pl.BlockSpec((BLOCK, 2 * LANES), lambda i: (at + i, 0)),
            pl.BlockSpec((BLOCK, 2 * LANES), lambda i: (at + i, 0)),
            pl.BlockSpec((1, BLOCK), lambda i: (0, at + i)),
            pl.BlockSpec((BLOCK, LANES), lambda i: (at + i, 0)),
        ],
        out_specs=[
            pl.BlockSpec((BLOCK, 2 * LANES), lambda i: (i, 0)),
            pl.BlockSpec((ORDER, BLOCK), lambda i: (0, i)),
        ],
        out_shape=[
            jax.ShapeDtypeStruct((width, 2 * LANES), F32),
            jax.ShapeDtypeStruct((ORDER, width), F32),
        ],
        scratch_shapes=[
            pltpu.VMEM((BLOCK, LANES), F32),
            pltpu.VMEM((2 * BLOCK, 2 * LANES), F32),
            pltpu.VMEM((2 * BLOCK, 6 * LANES), BF16),
        ],
        compiler_params=pltpu.CompilerParams(vmem_limit_bytes=VMEM_LIMIT),
        cost_estimate=pl.CostEstimate(
            flops=per * 2 * BLOCK * 768 * 256 * 2 * 8, bytes_accessed=per * 2_000_000, transcendentals=0
        ),
        name="pair",
    )(
        taps_flat, halo, halo, own, own, features, features, spectra[1:], long_spectra, fwd, inv,
        ends_hi, ends_lo, read_hi, read_lo, decay, skip,
    )


def gate_kernel(
    group_of, taps_ref, halo_q, own_q, x_q, h_ref, fwd_ref, inv_ref, read_hi, read_lo, local_ref,
    state_ref, out_ref, first_ref, freq_ref, prod_ref,
):
    step = pl.program_id(0)
    query = mediate(
        halo_q, own_q, x_q, taps_ref, group_of(step), h_ref, 0, fwd_ref[...], inv_ref[...],
        (first_ref, freq_ref, prod_ref),
    )
    pieces = jnp.concatenate(split_3(state_ref[...]), axis=0)
    spread = lax.dot_general(
        pieces, selector(3 * ORDER), (((0,), (0,)), ((), ())), preferred_element_type=F32
    )
    masked = jnp.where(same_group(), spread, 0.0)
    read = jnp.concatenate([read_hi[...], read_hi[...], read_lo[...]], axis=0)
    longed = local_ref[...] + dot_3(masked, read)
    out_ref[:, :LANES] = (query[:BLOCK] * longed[:, :LANES]).astype(BF16)
    out_ref[:, LANES:] = (query[BLOCK:] * longed[:, LANES:]).astype(BF16)


def gate_call(taps_flat, halo, own, features, spectra, fwd, inv, read_hi, read_lo, local, incoming, first, width, local_first):
    per = width // BLOCK
    at = first // BLOCK

    def group_of(step):
        return (at + step) * GROUPS

    buffer = pl.BlockSpec((ROWS, LANES), lambda i: (i, 0))
    return pl.pallas_call(
        functools.partial(gate_kernel, group_of),
        grid=(per,),
        in_specs=[
            pl.BlockSpec(memory_space=pltpu.SMEM),
            buffer,
            buffer,
            pl.BlockSpec((1, BLOCK, LANES), lambda i: (0, at + i, 0)),
            pl.BlockSpec((1, GROUPS, 2 * LANES), lambda i: (0, at + i, 0)),
            const_spec(fwd.shape),
            const_spec(inv.shape),
            pl.BlockSpec((BLOCK, 2 * LANES), lambda i: (at + i, 0)),
            pl.BlockSpec((BLOCK, 2 * LANES), lambda i: (at + i, 0)),
            pl.BlockSpec((BLOCK, 2 * LANES), lambda i: (at + i - local_first // BLOCK, 0)),
            pl.BlockSpec((ORDER, BLOCK), lambda i: (0, at + i)),
        ],
        out_specs=pl.BlockSpec((BLOCK, 2 * LANES), lambda i: (i, 0)),
        out_shape=jax.ShapeDtypeStruct((width, 2 * LANES), BF16),
        scratch_shapes=[
            pltpu.VMEM((BLOCK, LANES), F32),
            pltpu.VMEM((2 * BLOCK, 2 * LANES), F32),
            pltpu.VMEM((2 * BLOCK, 6 * LANES), BF16),
        ],
        compiler_params=pltpu.CompilerParams(vmem_limit_bytes=VMEM_LIMIT),
        cost_estimate=pl.CostEstimate(
            flops=per * 2 * BLOCK * 768 * 256 * 2 * 3, bytes_accessed=per * 1_000_000, transcendentals=0
        ),
        name="gate",
    )(
        taps_flat, halo, own, features, spectra, fwd, inv, read_hi, read_lo, local, incoming,
    )


def project_kernel(parts, half_ref, w_ref, *refs):
    out_ref = refs[-1]
    total = None
    at = 0
    for ref in refs[:-1]:
        width = ref.shape[0]
        term = dot(w_ref[:, at : at + width], ref[...])
        total = term if total is None else total + term
        at += width
    out_ref[...] = total


def project_call(weight, gated, half, halves):
    rows = weight.shape[0] // halves
    tile = min(rows, 256)
    steps = rows // tile
    return pl.pallas_call(
        functools.partial(project_kernel, len(gated)),
        grid_spec=pltpu.PrefetchScalarGridSpec(
            num_scalar_prefetch=1,
            grid=(steps,),
            in_specs=[
                pl.BlockSpec((tile, weight.shape[1]), lambda i, h: (h[0] * steps + i, 0)),
                *[pl.BlockSpec(g.shape, lambda i, h: (0, 0)) for g in gated],
            ],
            out_specs=pl.BlockSpec((tile, 2 * LANES), lambda i, h: (i, 0)),
        ),
        out_shape=jax.ShapeDtypeStruct((rows, 2 * LANES), F32),
        compiler_params=pltpu.CompilerParams(vmem_limit_bytes=VMEM_LIMIT),
        cost_estimate=pl.CostEstimate(
            flops=2 * rows * weight.shape[1] * 2 * LANES,
            bytes_accessed=rows * weight.shape[1] * 2,
            transcendentals=0,
        ),
        name="project",
    )(half, weight, *gated)


def split_xla(x):
    hi = lax.reduce_precision(x, 8, 7)
    return hi.astype(BF16), (x - hi).astype(BF16)


def plan(channels):
    units = channels // BLOCK
    if units >= 8:
        cuts = [units // 2, units // 4, units // 4]
    elif units >= 2:
        cuts = [units - units // 2, units // 2]
    else:
        cuts = [units]
    chunks, first = [], 0
    for cut in cuts:
        chunks.append((first * BLOCK, cut * BLOCK))
        first += cut
    return chunks


def exclusive_prefix(total, rates_wide, length):
    count, mine = lax.axis_size("seq"), lax.axis_index("seq")
    prefix = jnp.zeros_like(total)
    span = 1
    while span < count:
        upper = (mine // span) % 2 == 1
        last = 2 * span >= count
        route = [(i, i ^ span) for i in range(count) if not (last and (i // span) % 2 == 1)]
        other = lax.ppermute(total, "seq", route)
        steps_in = (mine % span).astype(F32)
        prefix = prefix + jnp.where(
            upper, jnp.exp(-rates_wide * (length * steps_in)) * other, 0.0
        )
        if not last:
            whole = jnp.exp(-rates_wide * float(length * span))
            total = jnp.where(upper, other * whole + total, total * whole + other)
        span *= 2
    return prefix


def per_device(features, short_filter, medium_filter, rates, residues, skip_gain, out_weight):
    channels, length = features.shape[1], features.shape[2]
    groups = rates.shape[0]
    fwd_np, inv_np = transforms()
    fwd = jnp.asarray(stacked(fwd_np))
    inv = jnp.asarray(stacked(inv_np))
    taps_flat = short_filter.reshape(-1)
    chunks = plan(channels)
    neighbours = [(i, i + 1) for i in range(lax.axis_size("seq") - 1)]

    pair_own = [send_call(features, taps_flat, (1, 2), *chunk) for chunk in chunks]
    query_own = [send_call(features, taps_flat, (0,), *chunk) for chunk in chunks]
    pair_halo = [lax.ppermute(own, "seq", neighbours) for own in pair_own]
    query_halo = [lax.ppermute(own, "seq", neighbours) for own in query_own]

    weight = residues * jnp.sqrt(-jnp.expm1(-2.0 * rates))
    steps = jnp.arange(length).astype(F32)
    read = weight[:, :, None] * jnp.exp(-rates[:, :, None] * (steps + 1.0))
    read_hi, read_lo = split_xla(read.reshape(groups * ORDER, length))
    rates_row = rates.reshape(1, groups * ORDER)
    back = (MEDIUM - 1.0) - jnp.arange(MEDIUM).astype(F32)
    ends_hi, ends_lo = split_xla(jnp.exp(-rates_row * back[:, None]))
    decay = jnp.exp(-rates_row * float(MEDIUM))
    kernel = jnp.sum(
        weight[:, :, None] * jnp.exp(-rates[:, :, None] * steps[:MEDIUM]), axis=1
    )
    filters = jnp.concatenate([medium_filter.reshape(-1, MEDIUM), kernel], axis=0)
    spectra = jnp.dot(
        filters, jnp.asarray(fwd_np[:MEDIUM].astype(np.float32)), precision=lax.Precision.HIGHEST
    ).reshape(4, groups, 2 * MEDIUM)
    skip = jnp.broadcast_to(skip_gain[:, None], (channels, LANES))
    tables = (ends_hi, ends_lo, read_hi, read_lo, decay, skip)
    rates_wide = jnp.repeat(rates.T, GROUP, axis=1)

    locals_, states = [], []
    for (first, width), halo, own in zip(chunks, pair_halo, pair_own):
        local, state = pair_call(
            taps_flat, halo, own, features, spectra[:3], spectra[3], fwd, inv, tables, first, width
        )
        locals_.append(local)
        states.append(state)
    incoming = exclusive_prefix(jnp.concatenate(states, axis=1), rates_wide, length)
    gated = [
        gate_call(
            taps_flat, halo, own, features, spectra, fwd, inv, read_hi, read_lo, local, incoming,
            first, width, first,
        )
        for (first, width), halo, own, local in zip(chunks, query_halo, query_own, locals_)
    ]
    if lax.axis_size("tp") == 2:
        me = lax.axis_index("tp").astype(jnp.int32).reshape(1)
        theirs = project_call(out_weight, gated, 1 - me, 2)
        arrived = lax.ppermute(theirs, "tp", [(0, 1), (1, 0)])
        return project_call(out_weight, gated, me, 2) + arrived
    full = project_call(out_weight, gated, jnp.zeros((1,), jnp.int32), 1)
    return lax.psum_scatter(full, "tp", scatter_dimension=0, tiled=True)


def solution(mesh):
    in_specs = (
        P(None, "tp", "seq"),
        P(None, "tp", None),
        P(None, "tp", None),
        P("tp", None),
        P("tp", None),
        P("tp"),
        P(None, "tp"),
    )
    out_specs = P("tp", "seq")
    return jax.shard_map(
        per_device, mesh=mesh, in_specs=in_specs, out_specs=out_specs, check_vma=False
    )
```

```python
import functools

import jax
import jax.numpy as jnp
import numpy as np
from jax import lax
from jax.experimental import pallas as pl
from jax.experimental.pallas import tpu as pltpu
from jax.sharding import PartitionSpec as P

GROUP = 16
SHORT = 7
MEDIUM = 128
ORDER = 16
LANES = 128
LENGTH = 256
POINTS = 512
BLOCK = 256
GROUPS = BLOCK // GROUP
BORDER = 16
ROWS = BLOCK + BORDER
VMEM_LIMIT = 20 * 1024 * 1024
BRIEF = pl.CostEstimate(flops=1, bytes_accessed=1, transcendentals=0)
SLOW = pl.CostEstimate(flops=1, bytes_accessed=100_000_000, transcendentals=0)
BF16 = jnp.bfloat16
F32 = jnp.float32


def split_np(x):
    hi = x.astype(np.float32).astype(jnp.bfloat16)
    lo = (x - hi.astype(np.float64)).astype(np.float32).astype(jnp.bfloat16)
    return hi, lo


def waves(tokens):
    k = np.arange(POINTS // 2)
    inner = (k % 4 == 1) | (k % 4 == 2)
    parts = []
    for chosen in (k[inner], k[~inner]):
        turns = ((2 * chosen + 1)[None, :] * np.asarray(tokens)[:, None]) % (2 * POINTS)
        angle = np.pi * turns / POINTS
        parts += [np.cos(angle), -np.sin(angle)]
    return np.concatenate(parts, axis=1)


def stacked(x):
    hi, lo = split_np(x)
    return np.concatenate([hi, hi, lo], axis=0)


def forward_stack():
    return stacked(waves(np.arange(LENGTH)))


def inverse_stack():
    return stacked((2.0 / POINTS) * waves(np.arange(LENGTH)).T)


def split(x):
    hi = x.astype(BF16)
    lo = (x - hi.astype(F32)).astype(BF16)
    return hi, lo


def split_3(x):
    hi = x.astype(BF16)
    rest = x - hi.astype(F32)
    mid = rest.astype(BF16)
    low = (rest - mid.astype(F32)).astype(BF16)
    return hi, mid, low


def dot(a, b):
    return jnp.dot(a, b, preferred_element_type=F32)


def dot_tn(a, b):
    return lax.dot_general(a, b, (((0,), (0,)), ((), ())), preferred_element_type=F32)


def dot_nt(a, b):
    return lax.dot_general(a, b, (((1,), (1,)), ((), ())), preferred_element_type=F32)


def rows_of(shape):
    return lax.broadcasted_iota(jnp.int32, shape, 0)


def lanes_of(shape):
    return lax.broadcasted_iota(jnp.int32, shape, 1)


def one_hot(condition):
    return condition.astype(F32).astype(BF16)


def join(x):
    hi, lo = split(x)
    return jnp.concatenate([hi, lo, hi], axis=1)


def const_spec(shape):
    return pl.BlockSpec(shape, lambda i: (0,) * len(shape))


def pinned(shape, dtype=F32):
    return pltpu.VMEM(shape, dtype)


def params():
    return pltpu.CompilerParams(vmem_limit_bytes=VMEM_LIMIT)


def send_kernel(blocks, outputs, x_ref, *refs):
    outs, (raw, staged, sems) = refs[-3 - outputs : -3], refs[-3:]
    reads, writes = [], []
    for j, (out, at, branch, first) in enumerate(blocks):
        read = pltpu.make_async_copy(
            x_ref.at[branch, pl.ds(first, BLOCK), :], raw.at[j], sems.at[0, j]
        )
        read.start()
        reads.append(read)
        writes.append(
            pltpu.make_async_copy(staged.at[j], outs[out].at[pl.ds(at, ROWS), :], sems.at[1, j])
        )
    for j in range(len(blocks)):
        reads[j].wait()
        staged[j, :BLOCK, :] = raw[j, :, LANES:]
        for b in range(BLOCK // LANES):
            tile = raw[j, b * LANES : (b + 1) * LANES, :LANES]
            staged[j, BLOCK + 8 * b : BLOCK + 8 * (b + 1), :] = tile.T[LANES - 8 :]
        writes[j].start()
    for write in writes:
        write.wait()


def send_call(features, chunks, after, cost=BRIEF):
    blocks, shapes = [], []
    for out, (branches, first, width) in enumerate(chunks):
        per = width // BLOCK
        for n, branch in enumerate(branches):
            for i in range(per):
                blocks.append((out, (n * per + i) * ROWS, branch, first + i * BLOCK))
        shapes.append(jax.ShapeDtypeStruct((len(branches) * per * ROWS, LANES), F32))
    anywhere = pl.BlockSpec(memory_space=pl.ANY)
    return pl.pallas_call(
        functools.partial(send_kernel, blocks, len(chunks)),
        grid=(1,),
        in_specs=[pl.BlockSpec(memory_space=pltpu.HBM)]
        + [pl.BlockSpec((8, LANES), lambda i: (0, 0))] * len(after),
        out_specs=[anywhere] * len(shapes),
        out_shape=shapes,
        scratch_shapes=[
            pltpu.VMEM((len(blocks), BLOCK, LENGTH), F32),
            pltpu.VMEM((len(blocks), ROWS, LANES), F32),
            pltpu.SemaphoreType.DMA((2, len(blocks))),
        ],
        compiler_params=params(),
        cost_estimate=cost,
        name="send",
    )(features, *after)


def tables_kernel(medium_ref, short_ref, rates_ref, weight_ref, fwd_ref, spectra_ref, wide_ref, line_ref):
    lag_hi = fwd_ref[:LENGTH]
    lag_lo = fwd_ref[2 * LENGTH :]
    stack = jnp.concatenate([lag_hi[:MEDIUM], lag_hi[:MEDIUM], lag_lo[:MEDIUM]], axis=0)
    short = jnp.concatenate([lag_hi[:16], lag_hi[:16], lag_lo[:16]], axis=0)
    for i in range(3):
        m = dot(join(medium_ref[i]), stack)
        hi, lo = split(short_ref[i])
        s = dot_tn(jnp.concatenate([hi, lo, hi], axis=0), short)
        for at in (0, LENGTH):
            re, im = slice(at, at + LANES), slice(at + LANES, at + LENGTH)
            spectra_ref[i, :, re] = m[:, re] * s[:, re] - m[:, im] * s[:, im]
            spectra_ref[i, :, im] = m[:, re] * s[:, im] + m[:, im] * s[:, re]
    groups = rates_ref.shape[1]
    time = rows_of((LENGTH, groups)).astype(F32)
    taps = jnp.zeros((LENGTH, groups), F32)
    for n in range(ORDER):
        taps = taps + weight_ref[n : n + 1, :] * jnp.exp(-rates_ref[n : n + 1, :] * time)
    hi, lo = split(taps)
    spectra_ref[3] = dot_tn(
        jnp.concatenate([hi, lo, hi], axis=0), jnp.concatenate([lag_hi, lag_hi, lag_lo], axis=0)
    )
    channels = wide_ref.shape[1]
    spread = one_hot(lanes_of((groups, channels)) // GROUP == rows_of((groups, channels)))
    mine = lanes_of((ORDER, channels)) % ORDER == rows_of((ORDER, channels))
    wide = sum(dot(piece, spread) for piece in split_3(rates_ref[...]))
    wide_ref[...] = wide
    weight = sum(dot(piece, spread) for piece in split_3(weight_ref[...]))
    line_ref[0:1, :] = jnp.sum(jnp.where(mine, wide, 0.0), axis=0, keepdims=True)
    line_ref[1:2, :] = jnp.sum(jnp.where(mine, weight, 0.0), axis=0, keepdims=True)
    line_ref[2:8, :] = jnp.zeros((6, channels), F32)


def tables_call(medium, short, rates, weight, fwd, channels):
    groups = rates.shape[1]
    return pl.pallas_call(
        tables_kernel,
        out_shape=[
            pinned((4, groups, POINTS), F32),
            pinned((ORDER, channels), F32),
            pinned((8, channels), F32),
        ],
        compiler_params=params(),
        cost_estimate=BRIEF,
        name="tables",
    )(medium, short, rates, weight, fwd)


def filtered(response, freq_ref, prod_ref, inv_ref):
    for r in range(freq_ref.shape[0] // BLOCK):
        for g in range(GROUPS):
            spectrum = response(r, g)
            rows = slice(r * BLOCK + g * GROUP, r * BLOCK + (g + 1) * GROUP)
            for at in (0, LENGTH):
                re, im = slice(at, at + LANES), slice(at + LANES, at + LENGTH)
                xr, xi, hr, hi = freq_ref[rows, re], freq_ref[rows, im], spectrum[:, re], spectrum[:, im]
                for part, y in ((re, xr * hr - xi * hi), (im, xr * hi + xi * hr)):
                    y_hi, y_lo = split(y)
                    prod_ref[rows, part] = y_hi
                    prod_ref[rows, POINTS + part.start : POINTS + part.stop] = y_lo
    terms = jnp.concatenate([prod_ref[...], prod_ref[:, :POINTS]], axis=1)
    return dot(terms, inv_ref[...])


def spectra_of(halo_ref, x_ref, row, plus_ref, minus_ref):
    select = one_hot(lanes_of((24, LANES)) == rows_of((24, LANES)) % 8 + LANES - 8)
    root = float(np.sqrt(2.0))
    for b in range(BLOCK // LANES):
        rows = slice(b * LANES, (b + 1) * LANES)
        to = slice(row + b * LANES, row + (b + 1) * LANES)
        edge = halo_ref[BLOCK + 8 * b : BLOCK + 8 * (b + 1), :]
        pack = jnp.concatenate([piece.astype(F32) for piece in split_3(edge)], axis=0)
        edge = dot_tn(pack.astype(BF16), select)
        edge = jnp.where(lanes_of(edge.shape) >= LANES - (SHORT - 2), edge, 0.0)
        halo, now, late = halo_ref[rows, :], x_ref[rows, :LANES], x_ref[rows, LANES:]
        low, high = now + edge, late - halo
        halo, edge = root * halo, root * edge
        for ref, parts in ((plus_ref, (low - halo, high + edge)), (minus_ref, (low + halo, high - edge))):
            for i, part in enumerate(parts):
                hi, lo = split(part)
                for j, piece in enumerate((hi, lo, hi)):
                    at = j * LENGTH + i * LANES
                    ref[to, at : at + LANES] = piece


def transform(plus_ref, minus_ref, fwd_ref, freq_ref):
    freq_ref[:, :LENGTH] = dot(plus_ref[...], fwd_ref[:, :LENGTH])
    freq_ref[:, LENGTH:] = dot(minus_ref[...], fwd_ref[:, LENGTH:])


def same_group():
    return rows_of((BLOCK, BLOCK)) // GROUP == lanes_of((BLOCK, BLOCK)) // ORDER


def fetched(x_ref, branch, first, steps, buffer, sems):
    def copy(i):
        return pltpu.make_async_copy(
            x_ref.at[branch, pl.ds(first + i * BLOCK, BLOCK), :], buffer.at[i], sems.at[i]
        )

    @pl.when(pl.program_id(0) == 0)
    def _():
        for i in range(steps):
            copy(i).start()

    return copy(pl.program_id(0))


def pair_kernel(
    first, steps, halo_k, halo_v, x_ref, spectra_ref, line_ref, skip_ref, fwd_ref, inv_ref,
    before_ref, local_ref, state_ref, plus_ref, minus_ref, freq_ref, prod_ref, freq_long, prod_long,
    keys, values, key_sems, value_sems,
):
    step = pl.program_id(0)
    fetches = (
        fetched(x_ref, 1, first, steps, keys, key_sems),
        fetched(x_ref, 2, first, steps, values, value_sems),
    )
    back = (LENGTH - 1 - rows_of((LENGTH, BLOCK))).astype(F32)
    decay_hi, decay_lo = split(jnp.exp(-line_ref[0:1, :] * back))
    for fetch in fetches:
        fetch.wait()
    spectra_of(halo_k, keys.at[step], 0, plus_ref, minus_ref)
    spectra_of(halo_v, values.at[step], BLOCK, plus_ref, minus_ref)
    transform(plus_ref, minus_ref, fwd_ref, freq_ref)
    mediated = filtered(lambda r, g: spectra_ref[1 + r, g : g + 1, :], freq_ref, prod_ref, inv_ref)
    product = mediated[:BLOCK] * mediated[BLOCK:]
    terms = join(product)
    freq_long[...] = dot(terms, fwd_ref[...])
    ends = dot(terms, jnp.concatenate([decay_hi, decay_hi, decay_lo], axis=0))
    local = filtered(lambda r, g: spectra_ref[3, g : g + 1, :], freq_long, prod_long, inv_ref)
    first_rows = rows_of((16, BLOCK))
    gain_hi, gain_mid, gain_low = (piece.astype(F32) for piece in split_3(skip_ref[...]))
    gain = jnp.where(
        first_rows == 0, gain_hi, jnp.where(first_rows == 1, gain_mid, jnp.where(first_rows == 2, gain_low, 0.0))
    )
    skip = dot_tn(gain.astype(BF16), jnp.ones((16, LENGTH), BF16))
    local_ref[...] = local + skip * product
    state = jnp.concatenate(split_3(jnp.where(same_group(), ends, 0.0)), axis=1)
    pick = one_hot(lanes_of((ORDER, BLOCK)) % ORDER == rows_of((ORDER, BLOCK)))
    columns = pl.ds(pl.multiple_of(first + step * BLOCK, BLOCK), BLOCK)
    state_ref[:, columns] = dot_nt(jnp.concatenate([pick, pick, pick], axis=1), state)

    if first:

        @pl.when(step == 0)
        def _():
            state_ref[:, :first] = before_ref[...]


def step_scratch(rows):
    return [
        pltpu.VMEM((rows, 3 * LENGTH), BF16),
        pltpu.VMEM((rows, 3 * LENGTH), BF16),
        pltpu.VMEM((rows, POINTS), F32),
        pltpu.VMEM((rows, 2 * POINTS), BF16),
    ]


def pair_call(halo, features, spectra, line, skip, fwd, inv, before, first, width):
    per = width // BLOCK
    at = first // BLOCK
    return pl.pallas_call(
        functools.partial(pair_kernel, first, per),
        grid=(per,),
        in_specs=[
            pl.BlockSpec((ROWS, LANES), lambda i: (i, 0)),
            pl.BlockSpec((ROWS, LANES), lambda i: (per + i, 0)),
            pl.BlockSpec(memory_space=pltpu.HBM),
            pl.BlockSpec((4, GROUPS, POINTS), lambda i: (0, at + i, 0)),
            pl.BlockSpec((8, BLOCK), lambda i: (0, at + i)),
            pl.BlockSpec((1, BLOCK), lambda i: (0, at + i)),
            const_spec(fwd.shape),
            const_spec(inv.shape),
            const_spec(before.shape),
        ],
        out_specs=[
            pl.BlockSpec((BLOCK, LENGTH), lambda i: (i, 0)),
            const_spec((ORDER, first + width)),
        ],
        out_shape=[
            pinned((width, LENGTH), F32),
            pinned((ORDER, first + width), F32),
        ],
        scratch_shapes=step_scratch(2 * BLOCK)
        + step_scratch(BLOCK)[2:]
        + [pltpu.VMEM((per, BLOCK, LENGTH), F32)] * 2
        + [pltpu.SemaphoreType.DMA((per,))] * 2,
        compiler_params=params(),
        cost_estimate=BRIEF,
        name="pair",
    )(halo, halo, features, spectra, line, skip, fwd, inv, before)


def query_kernel(
    first, steps, halo_q, x_ref, spectra_ref, fwd_ref, inv_ref,
    out_ref, plus_ref, minus_ref, freq_ref, prod_ref, queries, query_sems,
):
    fetched(x_ref, 0, first, steps, queries, query_sems).wait()
    spectra_of(halo_q, queries.at[pl.program_id(0)], 0, plus_ref, minus_ref)
    transform(plus_ref, minus_ref, fwd_ref, freq_ref)
    out_ref[...] = filtered(lambda r, g: spectra_ref[0, g : g + 1, :], freq_ref, prod_ref, inv_ref)


def query_call(halo, features, spectra, fwd, inv, first, width):
    per = width // BLOCK
    at = first // BLOCK
    return pl.pallas_call(
        functools.partial(query_kernel, first, per),
        grid=(per,),
        in_specs=[
            pl.BlockSpec((ROWS, LANES), lambda i: (i, 0)),
            pl.BlockSpec(memory_space=pltpu.HBM),
            pl.BlockSpec((1, GROUPS, POINTS), lambda i: (0, at + i, 0)),
            const_spec(fwd.shape),
            const_spec(inv.shape),
        ],
        out_specs=pl.BlockSpec((BLOCK, LENGTH), lambda i: (i, 0)),
        out_shape=pinned((width, LENGTH), F32),
        scratch_shapes=step_scratch(BLOCK)
        + [pltpu.VMEM((per, BLOCK, LENGTH), F32), pltpu.SemaphoreType.DMA((per,))],
        compiler_params=params(),
        cost_estimate=BRIEF,
        name="query",
    )(halo, features, spectra, fwd, inv)


def gate_kernel(locals_cut, queries_cut, prefix_ref, line_ref, *refs):
    local_refs, query_refs, out_ref = (
        refs[: len(locals_cut)], refs[len(locals_cut) : -1], refs[-1],
    )
    after = (rows_of((LENGTH, BLOCK)) + 1).astype(F32)
    pick = one_hot(lanes_of((3 * ORDER, BLOCK)) % ORDER == rows_of((3 * ORDER, BLOCK)) % ORDER)
    mask = same_group()

    def rows_from(cut, refs, at):
        for (first, width), ref in zip(cut, refs):
            if first <= at < first + width:
                return ref[at - first : at - first + BLOCK, :]

    for at in range(0, out_ref.shape[0], BLOCK):
        columns = slice(at, at + BLOCK)
        pieces = jnp.concatenate(split_3(prefix_ref[:, columns]), axis=0)
        spread = join(jnp.where(mask, dot_tn(pieces, pick), 0.0))
        read_hi, read_lo = split(line_ref[1:2, columns] * jnp.exp(-line_ref[0:1, columns] * after))
        longed = rows_from(locals_cut, local_refs, at) + dot_nt(
            spread, jnp.concatenate([read_hi, read_hi, read_lo], axis=1)
        )
        out_ref[columns, :] = (rows_from(queries_cut, query_refs, at) * longed).astype(BF16)


def gate_call(prefix, line, locals_, locals_cut, queries, queries_cut):
    inputs = [prefix, line, *locals_, *queries]
    channels = line.shape[1]
    return pl.pallas_call(
        functools.partial(gate_kernel, locals_cut, queries_cut),
        grid=(1,),
        in_specs=[pl.BlockSpec(x.shape, lambda i: (0, 0)) for x in inputs],
        out_specs=pl.BlockSpec((channels, LENGTH), lambda i: (0, 0)),
        out_shape=pinned((channels, LENGTH), BF16),
        compiler_params=params(),
        cost_estimate=BRIEF,
        name="gate",
    )(*inputs)


def project_kernel(half_ref, w_ref, gated_ref, out_ref):
    out_ref[...] = dot(w_ref[...], gated_ref[...])


def project_call(weight, gated, half, halves):
    rows = weight.shape[0] // halves
    tile = min(rows, 256)
    steps = rows // tile
    return pl.pallas_call(
        project_kernel,
        grid_spec=pltpu.PrefetchScalarGridSpec(
            num_scalar_prefetch=1,
            grid=(steps,),
            in_specs=[
                pl.BlockSpec(
                    (tile, weight.shape[1]),
                    lambda i, h: (h[0] * steps + i, 0),
                ),
                pl.BlockSpec(gated.shape, lambda i, h: (0, 0)),
            ],
            out_specs=pl.BlockSpec((tile, LENGTH), lambda i, h: (i, 0)),
        ),
        out_shape=jax.ShapeDtypeStruct((rows, LENGTH), F32),
        compiler_params=params(),
        cost_estimate=BRIEF,
        name="project",
    )(half, weight, gated)


def cut(channels, shares):
    units = channels // BLOCK
    if units < sum(shares):
        shares = [units - units // 2, units // 2] if units > 1 else [units]
    else:
        shares = [share * (units // sum(shares)) for share in shares]
    chunks, first = [], 0
    for share in shares:
        chunks.append((first * BLOCK, share * BLOCK))
        first += share
    return chunks


def merge_kernel(span, mine_ref, total_ref, other_ref, prefix_ref, rates_ref, _, out_prefix, out_total):
    other, rates = other_ref[...], rates_ref[...]
    upper = (mine_ref[0] // span) % 2 == 1
    lead = jnp.exp(-rates * (LENGTH * (mine_ref[0] % span)).astype(F32))
    whole = jnp.exp(-rates * float(LENGTH * span))
    out_prefix[...] = prefix_ref[...] + jnp.where(upper, lead, 0.0) * other
    out_total[...] = jnp.where(upper, other * whole + total_ref[...], total_ref[...] * whole + other)


def merge_call(span, mine, total, other, prefix, rates_wide, after):
    whole = pl.BlockSpec(total.shape, lambda i, m: (0, 0))
    return pl.pallas_call(
        functools.partial(merge_kernel, span),
        grid_spec=pltpu.PrefetchScalarGridSpec(
            num_scalar_prefetch=1,
            grid=(1,),
            in_specs=[whole] * 4 + [pl.BlockSpec((8, LANES), lambda i, m: (0, 0))],
            out_specs=[whole] * 2,
        ),
        out_shape=[pinned(total.shape), pinned(total.shape)],
        compiler_params=params(),
        cost_estimate=BRIEF,
        name="merge",
    )(mine, total, other, prefix, rates_wide, after)


def per_device(features, short_filter, medium_filter, rates, residues, skip_gain, out_weight):
    channels, length = features.shape[1], features.shape[2]
    fwd, inv = jnp.asarray(forward_stack()), jnp.asarray(inverse_stack())
    neighbours = [(i, i + 1) for i in range(lax.axis_size("seq") - 1)]
    pair_chunks = cut(channels, PAIR_SHARES)
    query_chunks = cut(channels, QUERY_SHARES)

    features = pltpu.with_memory_space_constraint(features, pltpu.HBM)
    pair_sent = send_call(features, [((1, 2), *pair_chunks[0])], ())
    pair_sent += send_call(
        features, [((1, 2), *chunk) for chunk in pair_chunks[1:]], pair_sent[:1], SLOW
    )
    pair_halo = [lax.ppermute(sent, "seq", neighbours) for sent in pair_sent]
    query_sent = send_call(
        features, [((0,), *chunk) for chunk in query_chunks], pair_sent[-1:], SLOW
    )
    weight = residues * jnp.sqrt(-jnp.expm1(-2.0 * rates))
    short = jnp.pad(jnp.swapaxes(short_filter, 1, 2), ((0, 0), (0, 16 - SHORT), (0, 0)))
    spectra, rates_wide, line = tables_call(
        medium_filter, short, rates.T, weight.T, fwd, channels
    )
    skip = skip_gain[None, :]
    fwd, inv = (pltpu.with_memory_space_constraint(x, pltpu.VMEM) for x in (fwd, inv))
    count = lax.axis_size("seq")
    mine = lax.axis_index("seq").astype(jnp.int32).reshape(1)
    locals_, state = [], line
    for chunk, halo in zip(pair_chunks, pair_halo):
        local, state = pair_call(halo, features, spectra, line, skip, fwd, inv, state, *chunk)
        locals_.append(local)
    query_halo = [lax.ppermute(sent, "seq", neighbours) for sent in query_sent]
    queries = [
        query_call(halo, features, spectra, fwd, inv, *chunk)
        for chunk, halo in zip(query_chunks, query_halo)
    ]
    total, prefix, span, n = state, jnp.zeros_like(state), 1, 0
    while span < count:
        other = lax.ppermute(total, "seq", [(i, i ^ span) for i in range(count) if i ^ span < count])
        after = queries[min(n, len(queries) - 2)] if n else query_halo[0]
        prefix, total = merge_call(span, mine, total, other, prefix, rates_wide, after)
        span, n = 2 * span, n + 1
    gated = gate_call(prefix, line, locals_, pair_chunks, queries, query_chunks)
    if lax.axis_size("tp") == 2:
        me = lax.axis_index("tp").astype(jnp.int32).reshape(1)
        theirs = project_call(out_weight, gated, 1 - me, 2)
        arrived = lax.ppermute(theirs, "tp", [(0, 1), (1, 0)])
        return project_call(out_weight, gated, me, 2) + arrived
    full = project_call(out_weight, gated, jnp.zeros((1,), jnp.int32), 1)
    return lax.psum_scatter(full, "tp", scatter_dimension=0, tiled=True)


PAIR_SHARES = [3, 2, 2, 1]
QUERY_SHARES = [2, 2, 2, 2]


def solution(mesh):
    in_specs = (
        P(None, "tp", "seq"),
        P(None, "tp", None),
        P(None, "tp", None),
        P("tp", None),
        P("tp", None),
        P("tp"),
        P(None, "tp"),
    )
    out_specs = P("tp", "seq")
    return jax.shard_map(
        per_device, mesh=mesh, in_specs=in_specs, out_specs=out_specs, check_vma=False
    )
```
